512 devices in a mesh: sensor: 4 (over z_lo), gx: 16 (over x, y), gy: 8 (over z_hi, core).
Axes of the slice: x: 4, y: 4, z: 16 (z_hi: 4, z_lo: 4; z = z_hi * 4 + z_lo), core: 2. Of those that a mesh axis runs over, the one named last changes fastest.
Arguments:
- adjoint_last: float32 [4, 64, 256, 1024], P('sensor', None, 'gx', 'gy'), may hold values from -6 to 6
- adjoint_prev: float32 [4, 64, 256, 1024], P('sensor', None, 'gx', 'gy'), may hold values from -6 to 6
- adjoint_source: float32 [4, 6], P('sensor'), may hold values from -8 to 8
- sensor_cell: int32 [4], P('sensor'), may hold values from 0 to 4194303
- sound_class: int32 [64, 256, 1024], P(None, 'gx', 'gy'), may hold values from 0 to 7
- depth_index: int32 [256, 1024], P('gx', 'gy'), may hold values from 16 to 64
Outputs:
- adjoint_field: float32 [4, 64, 256, 1024], P('sensor', None, 'gx', 'gy')
- surface: float32 [4, 256, 1024], P('sensor', 'gx', 'gy')
- hessian: float32 [16, 8, 4, 4], P('gx', 'gy', 'sensor')
The draws below stay inside these ranges and needn't reach their ends.
Inputs may be any that keep to these rules, and one draw needn't show every extreme that they name: `sensor_cell`: each sensor lies in the upper quarter of the levels, always in water.
All inputs are finite; a program needn't handle non-finite values.
Results may differ from the reference program's by a relative error of at most 0.0003.
Values sent between devices are 32-bit elements; how exact they have to be, the bound alone decides.
No kernel may reach another device: no remote copies, remote signals or barrier semaphores. Data moves between devices by JAX's collectives and lax.ppermute only.
A program may use at most 64 MiB of HBM per device.

```python
import jax
import jax.numpy as jnp
from jax import lax

NZ = 64
STEPS = 6
SENSORS = 4
NX = 256
NY = 1024
N_GX = 16
N_GY = 8


def plant(drawn, own_key, low, largest):
    longest = drawn.shape.index(max(drawn.shape))
    spots = []
    for shift in (0, 1):
        where = [jax.random.randint(jax.random.fold_in(own_key, axis), (), 0, length) for axis, length in enumerate(drawn.shape)]
        where[longest] = (where[longest] + shift) % drawn.shape[longest]
        spots.append(tuple(where))
    return drawn.at[spots[0]].set(low).at[spots[1]].set(largest)


def block_scale(own_key, dims, shards, low, largest):
    factor_of, own = 1.0, jax.random.fold_in(own_key, 6)
    for position, blocks in shards:
        draws = jnp.exp(jax.random.uniform(jax.random.fold_in(own, position), (blocks,), jnp.float32, low / len(shards), largest / len(shards)))
        factor_of = factor_of * jnp.repeat(draws, dims[position] // blocks).reshape([-1 if axis == position else 1 for axis in range(len(dims))])
    return factor_of


def scatter_about(own_key, extent, width, limit, split=(), kind=jnp.bfloat16):
    array = width * jax.random.normal(own_key, extent, jnp.float32)
    if split:
        array = array * block_scale(own_key, extent, split, -0.22, 0.18)
    return jnp.clip(array, -limit, limit).astype(kind)


def setup_inputs(seed: int = 0) -> dict:
    streams_of = jax.random.split(jax.random.key(seed), 7)
    return {
        "adjoint_last": scatter_about(streams_of[0], (SENSORS, NZ, NX, NY), 1.0, 6.0, ((0, 4), (2, 16), (3, 8)), jnp.float32),
        "adjoint_prev": scatter_about(streams_of[1], (SENSORS, NZ, NX, NY), 1.0, 6.0, ((0, 4), (2, 16), (3, 8)), jnp.float32),
        "adjoint_source": scatter_about(streams_of[2], (SENSORS, STEPS), 2.0, 8.0, ((0, 4),), jnp.float32),
        "sensor_cell": plant(jax.random.randint(streams_of[3], (SENSORS,), 0, NX * NY * (NZ // 4)), jax.random.fold_in(streams_of[3], 1), 0, (NX * NY * (NZ // 4)) - 1).astype(jnp.int32),
        "sound_class": plant(jax.random.randint(streams_of[4], (NZ, NX, NY), 0, 8), jax.random.fold_in(streams_of[4], 1), 0, 7).astype(jnp.int32),
        "depth_index": plant(jax.random.randint(streams_of[5], (NX, NY), NZ // 4, NZ + 1), jax.random.fold_in(streams_of[5], 1), NZ // 4, NZ).astype(jnp.int32),
    }


COURANT_SQUARED = (0.08, 0.11, 0.14, 0.17, 0.2, 0.23, 0.26, 0.3)
SURFACE_RATE = 0.3


def speeds(category_ids):
    result = jnp.zeros(category_ids.shape, jnp.float32)
    for category, amount in enumerate(COURANT_SQUARED):
        result = result + (category_ids == category).astype(jnp.float32) * amount
    return result


def advance(padded, before, coef, water, source):
    core = padded[..., 1:-1, 1:-1]
    field = core[..., 1:, :, :]
    top_level = core[..., 0, :, :]
    above = core[..., :-1, :, :]
    below = jnp.concatenate([field[..., 1:, :, :], jnp.zeros_like(field[..., :1, :, :])], axis=-3)
    sides = padded[..., 1:, 2:, 1:-1] + padded[..., 1:, :-2, 1:-1]
    sides = sides + padded[..., 1:, 1:-1, 2:] + padded[..., 1:, 1:-1, :-2]
    laplace = sides + above + below - 6.0 * field
    fresh = water * (2.0 * field - before + coef * laplace + source)
    top_new = top_level + SURFACE_RATE * (fresh[..., 0, :, :] - top_level)
    return fresh, top_new


def reference(adjoint_last, adjoint_prev, adjoint_source, sensor_cell, sound_class, depth_index):
    coef = speeds(sound_class)
    level_ids = lax.broadcasted_iota(jnp.int32, (NZ, NX, NY), 0)
    row_ids = lax.broadcasted_iota(jnp.int32, (NZ, NX, NY), 1)
    col_ids = lax.broadcasted_iota(jnp.int32, (NZ, NX, NY), 2)
    water = (level_ids < depth_index[None]).astype(jnp.float32)
    seabed = (level_ids == depth_index[None] - 1).astype(jnp.float32)
    global_ids = level_ids * (NX * NY) + row_ids * NY + col_ids

    def one_sensor(packed):
        last, prior, amounts, cell = packed
        hits = (global_ids == cell).astype(jnp.float32)
        state = jnp.concatenate([jnp.zeros((1, NX, NY), jnp.float32), last], 0)
        before = prior
        traces = []
        for instant in range(STEPS):
            padded = jnp.pad(state, ((0, 0), (1, 1), (1, 1)))
            fresh, top_new = advance(padded, before, coef, water, hits * amounts[instant])
            traces.append(jnp.sum(fresh * seabed, axis=0))
            before = state[1:]
            state = jnp.concatenate([top_new[None], fresh], 0)
        return state[1:], state[0], jnp.stack(traces, 0)

    fields, tops, traces = lax.map(one_sensor, (adjoint_last, adjoint_prev, adjoint_source, sensor_cell))
    tile_x = NX // N_GX
    tile_y = NY // N_GY
    shaped = traces.reshape(SENSORS, STEPS, N_GX, tile_x, N_GY, tile_y)
    hessian = jnp.einsum("anxiyj,bnxiyj->xyab", shaped, shaped, precision=lax.Precision.HIGHEST)
    hessian = hessian / (STEPS * tile_x * tile_y)
    return fields, tops, hessian
```

```python
import functools

import jax
import jax.numpy as jnp
from jax import lax
from jax.experimental import pallas as pl
from jax.experimental.pallas import tpu as pltpu
from jax.sharding import PartitionSpec as P

STEPS = 6
COURANT_SQUARED = (0.08, 0.11, 0.14, 0.17, 0.2, 0.23, 0.26, 0.3)
SURFACE_RATE = 0.3

NZ, TX, TY = 64, 16, 128
HALO = 4
ROWS = TX + 2 * HALO
TOP = 8
DEEP = NZ + 16
CHUNK = 16
STRIP = 11
ITEMS = (("p0", 1), ("p0", 2), ("old", 1), ("p1", 2), ("p1", 3), ("p2", 3), ("wc", 1), ("wc", 2), ("p2", 4), ("wc", 3))
VMEM = pl.BlockSpec(memory_space=pltpu.VMEM)
SMEM = pl.BlockSpec(memory_space=pltpu.SMEM)
F32 = jnp.float32


def lanes(rows):
    return lax.broadcasted_iota(jnp.int32, (rows, TY), 1)


def rolled(values, shift):
    shift = shift % TY
    return values if shift == 0 else pltpu.roll(values, shift, axis=1)


def swap_pairs(count, first):
    return [pair for i in range(first, count - 1, 2) for pair in ((i, i + 1), (i + 1, i))]


def pack_kernel(last, prev, kind, depth, p0, old, wc, near, far):
    even = lax.rem(lax.axis_index("gy"), 2) == 0
    lane = lanes(NZ)
    level = lax.broadcasted_iota(jnp.int32, (NZ, TY), 0)

    def half(h, carry):
        left = jnp.zeros((NZ, TY), F32)
        right = jnp.zeros((NZ, TY), F32)
        for j in range(8):
            x = h * 8 + j
            here = pl.ds(x, NZ, stride=TX)
            now, before, k = last[here, :], prev[here, :], kind[here, :]
            coef = jnp.full((NZ, TY), COURANT_SQUARED[0], F32)
            for category in range(1, 8):
                coef = jnp.where(k == category, COURANT_SQUARED[category], coef)
            coef = jnp.where(level < depth[pl.ds(x, 1), :], coef, 0.0)
            p0[x], old[x], wc[x] = now, before, coef
            base = 16 * j
            for values, start, width in ((now, base, 6), (before, base + 6, 5), (coef, base + 11, 5)):
                mine = (lane >= start) & (lane < start + width)
                left = jnp.where(mine, rolled(values, start), left)
                right = jnp.where(mine, rolled(values, start - (TY - width)), right)
        near[h] = jnp.where(even, right, left)
        far[h] = jnp.where(even, left, right)
        return carry

    lax.fori_loop(0, 2, half, 0)


def update_row(now, old, wc, out, row, old_row, wc_row, out_row, depth_row=None):
    lane = lanes(CHUNK)
    trace = jnp.zeros((CHUNK, TY), F32)
    for start in range(0, NZ, CHUNK):
        at = pl.ds(TOP + start, CHUNK)
        centre = [now[row, t, at, :] for t in (0, 1)]
        down = [pltpu.roll(c, 1, axis=1) for c in centre]
        up = [pltpu.roll(c, TY - 1, axis=1) for c in centre]
        for t in (0, 1):
            beside = jnp.where(lane == 0, down[1 - t], down[t]) + jnp.where(lane == TY - 1, up[1 - t], up[t])
            rows = now[row - 1, t, at, :] + now[row + 1, t, at, :]
            levels = now[row, t, pl.ds(TOP + start - 1, CHUNK), :] + now[row, t, pl.ds(TOP + start + 1, CHUNK), :]
            laplace = (rows + beside) + levels - 6.0 * centre[t]
            coef = wc(wc_row, t, pl.ds(start, CHUNK))
            fresh = 2.0 * centre[t] - old(old_row, t, start) + coef * laplace
            fresh = jnp.where(coef > 0.0, fresh, 0.0)
            out[out_row, t, at, :] = fresh
            if t == 0 and depth_row is not None:
                level = lax.broadcasted_iota(jnp.int32, (CHUNK, TY), 0) + start
                trace = trace + jnp.where(level == depth_row - 1, fresh, 0.0)
            if start == 0:
                eta = now[row, t, TOP - 1 : TOP, :]
                out[out_row, t, TOP - 1 : TOP, :] = eta + SURFACE_RATE * (fresh[0:1] - eta)
    return jnp.sum(trace, axis=0, keepdims=True)


def sensor_place(cell):
    number = cell[0]
    size_y = TY * lax.axis_size("gy")
    plane = TX * lax.axis_size("gx") * size_y
    z = lax.div(number, plane)
    x = lax.div(lax.rem(number, plane), size_y) - TX * lax.axis_index("gx")
    y = lax.rem(number, size_y) - TY * lax.axis_index("gy")
    tile = jnp.where((y >= 0) & (y < TY), 0, 1)
    lane = lax.rem(y + 2 * size_y, TY)
    return z, x, tile, lane, (y >= -5) & (y < TY + 5)


def inject(out, row, place, amount):
    z, _, tile, lane, _ = place
    hit = jnp.where(lanes(1) == lane, amount, 0.0)
    at = pl.ds(TOP + z, 1)
    out[row, tile, at, :] = out[row, tile, at, :] + hit
    top = pl.ds(TOP - 1, 1)
    out[row, tile, top, :] = out[row, tile, top, :] + jnp.where(z == 0, SURFACE_RATE, 0.0) * hit
    return hit


def edge_kernel(p0, old, wc, near, far, cell, source, strip_a, strip_b, aux_p, aux_o, aux_w, e0, e1, e2):
    even = lax.rem(lax.axis_index("gy"), 2) == 0
    lane = lanes(NZ)
    for ref in (e0, e1):
        for x in range(TX):
            for t in (0, 1):
                ref[x, t, 0:TOP, :] = jnp.zeros((TOP, TY), F32)
                ref[x, t, TOP + NZ :, :] = jnp.zeros((8, TY), F32)

    def half(h, carry):
        from_right = jnp.where(even, near[h], far[h])
        from_left = jnp.where(even, far[h], near[h])
        for j in range(8):
            x = h * 8 + j
            base = 16 * j
            for ref, start, width in ((aux_p, base, 6), (aux_o, base + 6, 5), (aux_w, base + 11, 5)):
                right = rolled(from_right, -start)
                left = rolled(from_left, TY - width - start)
                ref[x] = jnp.where(lane < width, right, jnp.where(lane >= TY - width, left, 0.0))
            e0[x, 0, TOP : TOP + NZ, :] = p0[x]
            e0[x, 1, TOP : TOP + NZ, :] = aux_p[x]
        return carry

    lax.fori_loop(0, 2, half, 0)

    def old_0(x, t, start):
        return (old, aux_o)[t][x, pl.ds(start, CHUNK), :]

    def old_1(x, t, start):
        return e0[x, t, pl.ds(TOP + start, CHUNK), :]

    def coef(x, t, at):
        return (wc, aux_w)[t][x, at, :]

    place = sensor_place(cell)
    x_s, here = place[1], place[4]

    def first(i, carry):
        x = jnp.where(i < 4, 1 + i, 7 + i)
        update_row(e0, old_0, coef, e1, x, x, x, x)
        return carry

    lax.fori_loop(0, 8, first, 0)
    inside = here & (((x_s >= 1) & (x_s <= 4)) | ((x_s >= 11) & (x_s <= 14)))
    inject(e1, jnp.clip(x_s, 0, TX - 1), place, jnp.where(inside, source[0, 0], 0.0))

    def second(i, carry):
        x = jnp.where(i < 2, 2 + i, 10 + i)
        update_row(e1, old_1, coef, e2, x, x, x, x)
        return carry

    lax.fori_loop(0, 4, second, 0)
    inside = here & (((x_s >= 2) & (x_s <= 3)) | ((x_s >= 12) & (x_s <= 13)))
    inject(e2, jnp.clip(x_s, 0, TX - 1), place, jnp.where(inside, source[0, 1], 0.0))

    body = slice(TOP, TOP + NZ)
    upper_a = lax.rem(lax.axis_index("gx"), 2) == 0
    for strip, upper in ((strip_a, upper_a), (strip_b, ~upper_a)):
        corner = jnp.zeros((NZ, TY), F32)
        for k, (name, d) in enumerate(ITEMS):
            x = jnp.where(upper, TX - d, d - 1)
            if name == "old":
                main, aux = old[x], aux_o[x]
            elif name == "wc":
                main, aux = wc[x], aux_w[x]
            else:
                ref = {"p0": e0, "p1": e1, "p2": e2}[name]
                main, aux = ref[x, 0, body, :], ref[x, 1, body, :]
            strip[k] = main
            if k < 8:
                corner = jnp.where((lane >= 16 * k) & (lane < 16 * k + 16), rolled(aux, 8 + 16 * k), corner)
        strip[STRIP - 1] = corner


def steps_kernel(p0, old, wc, aux_p, aux_o, aux_w, strip_a, strip_b, depth, cell, source,
                 field, surface, trace, levels, coefs, depths, traces):
    body = slice(TOP, TOP + NZ)
    lane = lanes(NZ)
    depths[...] = jnp.zeros((ROWS, TY), jnp.int32)
    depths[HALO : HALO + TX, :] = depth[...]

    def blank(row, carry):
        for k in range(3):
            for t in (0, 1):
                levels[k, row, t, 0:TOP, :] = jnp.zeros((TOP, TY), F32)
                levels[k, row, t, TOP + NZ :, :] = jnp.zeros((8, TY), F32)
        return carry

    lax.fori_loop(0, ROWS, blank, 0)

    def fill(x, carry):
        row = x + HALO
        levels[1, row, 0, body, :] = p0[x]
        levels[1, row, 1, body, :] = aux_p[x]
        levels[0, row, 0, body, :] = old[x]
        levels[0, row, 1, body, :] = aux_o[x]
        coefs[row, 0] = wc[x]
        coefs[row, 1] = aux_w[x]
        return carry

    lax.fori_loop(0, TX, fill, 0)

    upper_a = lax.rem(lax.axis_index("gx"), 2) == 0
    for strip, upper in ((strip_a, upper_a), (strip_b, ~upper_a)):
        corner = strip[STRIP - 1]
        for k, (name, d) in enumerate(ITEMS):
            row = jnp.where(upper, HALO + TX - 1 + d, HALO - d)
            main = strip[k]
            if k < 8:
                aux = jnp.where((lane < 8) | (lane >= TY - 8), rolled(corner, -(8 + 16 * k)), 0.0)
            else:
                aux = jnp.zeros((NZ, TY), F32)
            for t, values in ((0, main), (1, aux)):
                if name == "wc":
                    coefs[row, t] = values
                    continue
                slot = {"old": 0, "p0": 1, "p1": 2, "p2": 0}[name]
                levels[slot, row, t, body, :] = values
                if name == "p1":
                    levels[2, row, t, TOP - 1 : TOP, :] = SURFACE_RATE * values[0:1]
                if name == "p2" and d == 3:
                    eta = levels[2, row, t, TOP - 1 : TOP, :]
                    levels[0, row, t, TOP - 1 : TOP, :] = eta + SURFACE_RATE * (values[0:1] - eta)

    place = sensor_place(cell)
    z_s, x_s, tile, _, here = place

    def coef(row, t, at):
        return coefs[row, t, at, :]

    for n, reach in zip(range(1, STEPS + 1), (1, 2, 3, 2, 1, 0)):
        now, before, out = levels.at[n % 3], levels.at[(n - 1) % 3], levels.at[(n + 1) % 3]

        def old_at(row, t, start):
            return before[row, t, pl.ds(TOP + start, CHUNK), :]

        def one(row, carry):
            sums = update_row(now, old_at, coef, out, row, row, row, row, depths[pl.ds(row, 1), :])
            traces[n - 1, pl.ds(row, 1), :] = sums
            return carry

        lax.fori_loop(HALO - reach, HALO + TX + reach, one, 0)
        inside = here & (x_s >= -reach) & (x_s < TX + reach)
        row_s = jnp.clip(x_s + HALO, 0, ROWS - 1)
        hit = inject(out, row_s, place, jnp.where(inside, source[0, n - 1], 0.0))
        at = pl.ds(row_s, 1)
        seabed = (depths[at, :] - 1 == z_s) & (tile == 0)
        traces[n - 1, at, :] = traces[n - 1, at, :] + jnp.where(seabed, hit, 0.0)

    final = levels.at[(STEPS + 1) % 3]

    def give(x, carry):
        field[pl.ds(x, NZ, stride=TX), :] = final[x + HALO, 0, body, :]
        surface[pl.ds(x, 1), :] = final[x + HALO, 0, TOP - 1 : TOP, :]
        return carry

    lax.fori_loop(0, TX, give, 0)
    for n in range(STEPS):
        rows = traces[n, HALO : HALO + TX, :]
        for s in range(trace.shape[0]):
            trace[s, n * TX : (n + 1) * TX, :] = rows


def shape(*dims):
    return jax.ShapeDtypeStruct(dims, F32)


def cost(flops, moved):
    return pl.CostEstimate(flops=flops, bytes_accessed=moved, transcendentals=0)


def on_device(adjoint_last, adjoint_prev, adjoint_source, sensor_cell, sound_class, depth_index):
    sensors = lax.axis_size("sensor")
    count_x, count_y = lax.axis_size("gx"), lax.axis_size("gy")
    params = pltpu.CompilerParams(vmem_limit_bytes=40 * 2**20)
    flat = (NZ * TX, TY)
    block = (TX, NZ, TY)
    p0, old, wc, near, far = pl.pallas_call(
        pack_kernel,
        out_shape=[shape(*block)] * 3 + [shape(2, NZ, TY)] * 2,
        in_specs=[VMEM] * 4,
        out_specs=[VMEM] * 5,
        compiler_params=params,
        name="pack_columns",
    )(adjoint_last.reshape(flat), adjoint_prev.reshape(flat), sound_class.reshape(flat), depth_index)
    far = lax.ppermute(far, "gy", swap_pairs(count_y, 1))
    near = lax.ppermute(near, "gy", swap_pairs(count_y, 0))
    padded = (TX, 2, DEEP, TY)
    strip_a, strip_b, aux_p, aux_o, aux_w = pl.pallas_call(
        edge_kernel,
        out_shape=[shape(STRIP, NZ, TY)] * 2 + [shape(*block)] * 3,
        in_specs=[VMEM] * 5 + [SMEM] * 2,
        out_specs=[VMEM] * 5,
        scratch_shapes=[pltpu.VMEM(padded, F32)] * 3,
        compiler_params=params,
        name="edge_rows",
    )(p0, old, wc, near, far, sensor_cell, adjoint_source)
    strip_a = lax.ppermute(strip_a, "gx", swap_pairs(count_x, 0))
    strip_b = lax.ppermute(strip_b, "gx", swap_pairs(count_x, 1))
    field, surface, trace = pl.pallas_call(
        steps_kernel,
        out_shape=[shape(*flat), shape(TX, TY), shape(sensors, STEPS * TX, TY)],
        in_specs=[VMEM] * 9 + [SMEM] * 2,
        out_specs=[VMEM] * 3,
        scratch_shapes=[
            pltpu.VMEM((3, ROWS, 2, DEEP, TY), F32),
            pltpu.VMEM((ROWS, 2, NZ, TY), F32),
            pltpu.VMEM((ROWS, TY), jnp.int32),
            pltpu.VMEM((STEPS, ROWS, TY), F32),
        ],
        compiler_params=params,
        name="six_steps",
    )(p0, old, wc, aux_p, aux_o, aux_w, strip_a, strip_b, depth_index, sensor_cell, adjoint_source)
    others = lax.all_to_all(trace, "sensor", 0, 0)
    gram = jnp.sum(trace[0][None] * others, axis=(1, 2)) / (STEPS * TX * TY)
    return field.reshape(1, NZ, TX, TY), surface[None], gram.reshape(1, 1, 1, sensors)


def solution(mesh):
    return jax.shard_map(
        on_device,
        mesh=mesh,
        in_specs=(
            P("sensor", None, "gx", "gy"),
            P("sensor", None, "gx", "gy"),
            P("sensor", None),
            P("sensor"),
            P(None, "gx", "gy"),
            P("gx", "gy"),
        ),
        out_specs=(
            P("sensor", None, "gx", "gy"),
            P("sensor", "gx", "gy"),
            P("gx", "gy", "sensor", None),
        ),
        check_vma=False,
    )
```

```python
import functools

import jax
import jax.numpy as jnp
from jax import lax
from jax.experimental import pallas as pl
from jax.experimental.pallas import tpu as pltpu
from jax.sharding import PartitionSpec as P

STEPS = 6
COURANT_SQUARED = (0.08, 0.11, 0.14, 0.17, 0.2, 0.23, 0.26, 0.3)
SURFACE_RATE = 0.3

NZ, TX, TY = 64, 16, 128
HALO = 4
ROWS = TX + 2 * HALO
TOP = 8
DEEP = NZ + 16
CHUNK = 16
STRIP = 11
ITEMS = (("p0", 1), ("p0", 2), ("old", 1), ("p1", 2), ("p1", 3), ("p2", 3), ("wc", 1), ("wc", 2), ("p2", 4), ("wc", 3))
VMEM = pl.BlockSpec(memory_space=pltpu.VMEM)
SMEM = pl.BlockSpec(memory_space=pltpu.SMEM)
HBM = pl.BlockSpec(memory_space=pltpu.HBM)
F32 = jnp.float32


def lanes(rows):
    return lax.broadcasted_iota(jnp.int32, (rows, TY), 1)


def rolled(values, shift):
    shift = shift % TY
    return values if shift == 0 else pltpu.roll(values, shift, axis=1)


def swap_pairs(count, first):
    return [pair for i in range(first, count - 1, 2) for pair in ((i, i + 1), (i + 1, i))]


def pack_kernel(last, prev, kind, depth, p0, old, wc, near, far, depth_out, now_v, prev_v, kind_v, sems):
    copies = [
        pltpu.make_async_copy(src, dst, sems.at[i])
        for i, (src, dst) in enumerate(((last, now_v), (prev, prev_v), (kind, kind_v), (depth, depth_out)))
    ]
    for copy in copies:
        copy.start()
    even = lax.rem(lax.axis_index("gy"), 2) == 0
    lane = lanes(NZ)
    level = lax.broadcasted_iota(jnp.int32, (NZ, TY), 0)
    for copy in copies:
        copy.wait()

    def half(h, carry):
        left = jnp.zeros((NZ, TY), F32)
        right = jnp.zeros((NZ, TY), F32)
        for j in range(8):
            x = h * 8 + j
            here = pl.ds(x, NZ, stride=TX)
            now, before, k = now_v[here, :], prev_v[here, :], kind_v[here, :]
            coef = jnp.full((NZ, TY), COURANT_SQUARED[0], F32)
            for category in range(1, 8):
                coef = jnp.where(k == category, COURANT_SQUARED[category], coef)
            coef = jnp.where(level < depth_out[pl.ds(x, 1), :], coef, 0.0)
            p0[x], old[x], wc[x] = now, before, coef
            base = 16 * j
            for values, start, width in ((now, base, 6), (before, base + 6, 5), (coef, base + 11, 5)):
                mine = (lane >= start) & (lane < start + width)
                left = jnp.where(mine, rolled(values, start), left)
                right = jnp.where(mine, rolled(values, start - (TY - width)), right)
        near[h] = jnp.where(even, right, left)
        far[h] = jnp.where(even, left, right)
        return carry

    lax.fori_loop(0, 2, half, 0)


def update_row(now, old, wc, out, row, depth_row=None, trace=None, tiles=(0, 1)):
    lane = lanes(CHUNK)
    results = []
    total = jnp.zeros((8, TY), F32)
    for start in range(0, NZ, CHUNK):
        at = pl.ds(TOP + start, CHUNK)
        centre = [now[row, t, at, :] for t in (0, 1)]
        down = [pltpu.roll(c, 1, axis=1) for c in centre]
        up = [pltpu.roll(c, TY - 1, axis=1) for c in centre]
        for t in tiles:
            beside = jnp.where(lane == 0, down[1 - t], down[t]) + jnp.where(lane == TY - 1, up[1 - t], up[t])
            rows = now[row - 1, t, at, :] + now[row + 1, t, at, :]
            levels = now[row, t, pl.ds(TOP + start - 1, CHUNK), :] + now[row, t, pl.ds(TOP + start + 1, CHUNK), :]
            laplace = (rows + beside) + levels - 6.0 * centre[t]
            coef = wc[row, t, pl.ds(start, CHUNK), :]
            fresh = 2.0 * centre[t] - old[row, t, at, :] + coef * laplace
            fresh = jnp.where(coef > 0.0, fresh, 0.0)
            results.append((t, at, fresh))
            if t == 0 and depth_row is not None:
                level = lax.broadcasted_iota(jnp.int32, (CHUNK, TY), 0) + start
                bed = jnp.where(level == depth_row - 1, fresh, 0.0)
                for part in range(0, CHUNK, 8):
                    total = total + bed[part : part + 8]
    top = pl.ds(TOP - 1, 1)
    etas = []
    for t in tiles:
        eta = now[row, t, top, :]
        etas.append(eta + SURFACE_RATE * (results[t][2][0:1] - eta))
    for t, at, fresh in results:
        out[row, t, at, :] = fresh
    for t in tiles:
        out[row, t, top, :] = etas[t]
        out[row, t, TOP + NZ : TOP + NZ + 1, :] = jnp.zeros((1, TY), F32)
    if trace is not None:
        trace[row - HALO] = total


def fetch(source, source_s, sem):
    copy = pltpu.make_async_copy(source, source_s, sem)
    copy.start()
    return copy


def sensor_place(cell):
    number = cell[0]
    size_y = TY * lax.axis_size("gy")
    plane = TX * lax.axis_size("gx") * size_y
    z = lax.div(number, plane)
    x = lax.div(lax.rem(number, plane), size_y) - TX * lax.axis_index("gx")
    y = lax.rem(number, size_y) - TY * lax.axis_index("gy")
    tile = jnp.where((y >= 0) & (y < TY), 0, 1)
    lane = lax.rem(y + 2 * size_y, TY)
    return z, x, tile, lane, (y >= -5) & (y < TY + 5)


def inject(out, place, amount, first, end, depth, trace):
    z, x, tile, lane, here = place
    inner = jnp.minimum(x, TX - 1 - x)
    amount = jnp.where(here & (inner >= first) & (inner < end), amount, 0.0)
    hit = jnp.where(lanes(1) == lane, amount, 0.0)
    row = jnp.clip(x + HALO, 0, ROWS - 1)
    at = pl.ds(TOP + z, 1)
    out[row, tile, at, :] = out[row, tile, at, :] + hit
    top = pl.ds(TOP - 1, 1)
    out[row, tile, top, :] = out[row, tile, top, :] + jnp.where(z == 0, SURFACE_RATE, 0.0) * hit
    own = jnp.clip(x, 0, TX - 1)
    bed = (depth[pl.ds(own, 1), :] - 1 == z) & (tile == 0) & (inner >= 0)
    trace[own, 0:1, :] = trace[own, 0:1, :] + jnp.where(bed, hit, 0.0)


def own_rows(now, old, wc, out, first, end, depth, trace, tiles=(0, 1)):
    def pair(x, carry):
        for y in (x, TX - 1 - x):
            update_row(now, old, wc, out, y + HALO, depth[pl.ds(y, 1), :], trace, tiles)
        return carry

    lax.fori_loop(first, end, pair, 0)


def clear_ends(ref, row, t):
    ref[row, t, 0:TOP, :] = jnp.zeros((TOP, TY), F32)
    ref[row, t, TOP + NZ :, :] = jnp.zeros((8, TY), F32)


def edge_kernel(p0, old, wc, near, far, depth, cell, source, strip_a, strip_b, l0, lold, w, l1, l2, trace,
                source_s, sem):
    copy = fetch(source, source_s, sem)
    even = lax.rem(lax.axis_index("gy"), 2) == 0
    lane = lanes(NZ)
    body = slice(TOP, TOP + NZ)

    def half(h, carry):
        from_right = jnp.where(even, near[h], far[h])
        from_left = jnp.where(even, far[h], near[h])
        for j in range(8):
            x = h * 8 + j
            row = x + HALO
            base = 16 * j
            aux = []
            for start, width in ((base, 6), (base + 6, 5), (base + 11, 5)):
                right = rolled(from_right, -start)
                left = rolled(from_left, TY - width - start)
                aux.append(jnp.where(lane < width, right, jnp.where(lane >= TY - width, left, 0.0)))
            l0[row, 0, body, :], lold[row, 0, body, :], w[row, 0] = p0[x], old[x], wc[x]
            l0[row, 1, body, :], lold[row, 1, body, :], w[row, 1] = aux
            for t in (0, 1):
                clear_ends(l0, row, t)
        return carry

    lax.fori_loop(0, 2, half, 0)
    copy.wait()
    place = sensor_place(cell)
    own_rows(l0, lold, w, l1, 1, 5, depth, trace.at[0])
    inject(l1, place, source_s[0, 0], 1, 5, depth, trace.at[0])
    own_rows(l1, l0, w, l2, 2, 4, depth, trace.at[1])
    inject(l2, place, source_s[0, 1], 2, 4, depth, trace.at[1])

    upper_a = lax.rem(lax.axis_index("gx"), 2) == 0
    for strip, upper in ((strip_a, upper_a), (strip_b, ~upper_a)):
        corner = jnp.zeros((NZ, TY), F32)
        for k, (name, d) in enumerate(ITEMS):
            row = HALO + jnp.where(upper, TX - d, d - 1)
            if name == "wc":
                main, aux = w[row, 0], w[row, 1]
            else:
                ref = {"old": lold, "p0": l0, "p1": l1, "p2": l2}[name]
                main, aux = ref[row, 0, body, :], ref[row, 1, body, :]
            strip[k] = main
            if k < 8:
                corner = jnp.where((lane >= 16 * k) & (lane < 16 * k + 16), rolled(aux, 8 + 16 * k), corner)
        strip[STRIP - 1] = corner


def inner_kernel(l0, lold, w, l1_in, l2_in, trace_in, depth, cell, source, l1, l2, trace, l3, l4, l5, l6,
                 source_s, sem):
    copy = fetch(source, source_s, sem)
    copy.wait()
    place = sensor_place(cell)
    steps = [lold, l0, l1, l2, l3, l4, l5, l6]
    for n, first in zip(range(1, STEPS + 1), (5, 4, 3, 4, 5, 6)):
        now, old, out = steps[n], steps[n - 1], steps[n + 1]
        own_rows(now, old, w, out, first, TX // 2, depth, trace.at[n - 1], (0, 1) if n < STEPS else (0,))
        inject(out, place, source_s[0, n - 1], first, TX // 2, depth, trace.at[n - 1])


def frontier_kernel(l0_in, lold_in, w_in, l1_in, l2_in, l3_in, l4_in, l5_in, l6_in, trace_in, strip_a, strip_b, depth, cell, source,
                    l0, lold, w, l1, l2, l3, l4, l5, l6, trace, mine, others, source_s, sem):
    copy = fetch(source, source_s, sem)
    body = slice(TOP, TOP + NZ)
    lane = lanes(NZ)
    top = slice(TOP - 1, TOP)
    upper_a = lax.rem(lax.axis_index("gx"), 2) == 0
    for strip, upper in ((strip_a, upper_a), (strip_b, ~upper_a)):
        corner = strip[STRIP - 1]
        for k, (name, d) in enumerate(ITEMS):
            row = jnp.where(upper, HALO + TX - 1 + d, HALO - d)
            if k < 8:
                aux = jnp.where((lane < 8) | (lane >= TY - 8), rolled(corner, -(8 + 16 * k)), 0.0)
            else:
                aux = jnp.zeros((NZ, TY), F32)
            for t, values in ((0, strip[k]), (1, aux)):
                if name == "wc":
                    w[row, t] = values
                    continue
                ref = {"old": lold, "p0": l0, "p1": l1, "p2": l2}[name]
                clear_ends(ref, row, t)
                ref[row, t, body, :] = values
                if name == "p1":
                    l1[row, t, top, :] = SURFACE_RATE * values[0:1]
                if name == "p2" and d == 3:
                    eta = l1[row, t, top, :]
                    l2[row, t, top, :] = eta + SURFACE_RATE * (values[0:1] - eta)
    copy.wait()
    place = sensor_place(cell)
    steps = [lold, l0, l1, l2, l3, l4, l5, l6]
    for n, reach in zip(range(1, STEPS + 1), (1, 2, 3, 2, 1, 0)):
        now, old, out = steps[n], steps[n - 1], steps[n + 1]
        own_rows(now, old, w, out, 0, n, depth, trace.at[n - 1], (0, 1) if n < STEPS else (0,))

        def halo_pair(d, carry):
            for row in (HALO - d, HALO + TX - 1 + d):
                update_row(now, old, w, out, row)
            return carry

        if reach:
            lax.fori_loop(1, reach + 1, halo_pair, 0)
        inject(out, place, source_s[0, n - 1], -reach, n, depth, trace.at[n - 1])
    for n in range(STEPS):
        rows = jnp.sum(trace[n], axis=1)
        mine[n * TX : (n + 1) * TX, :] = rows * (1.0 / (STEPS * TX * TY))
        for s in range(others.shape[0]):
            others[s, n * TX : (n + 1) * TX, :] = rows


def give_kernel(final, field, surface):
    def give(x, carry):
        field[pl.ds(x, NZ, stride=TX), :] = final[x + HALO, 0, TOP : TOP + NZ, :]
        surface[pl.ds(x, 1), :] = final[x + HALO, 0, TOP - 1 : TOP, :]
        return carry

    lax.fori_loop(0, TX, give, 0)


def shape(*dims):
    return jax.ShapeDtypeStruct(dims, F32)


def cost(rows, moved):
    return pl.CostEstimate(flops=rows * NZ * TY * 16, bytes_accessed=moved, transcendentals=0)


SMALL = [pltpu.SMEM((1, STEPS), F32), pltpu.SemaphoreType.DMA]


def on_device(adjoint_last, adjoint_prev, adjoint_source, sensor_cell, sound_class, depth_index):
    sensors = lax.axis_size("sensor")
    count_x, count_y = lax.axis_size("gx"), lax.axis_size("gy")
    params = pltpu.CompilerParams(vmem_limit_bytes=8 * 2**20)
    flat = (NZ * TX, TY)
    block = (TX, NZ, TY)
    fields = [a.reshape(flat) for a in (adjoint_last, adjoint_prev, sound_class)]
    fields = [pltpu.with_memory_space_constraint(a, pltpu.HBM) for a in (*fields, depth_index)]
    adjoint_source = pltpu.with_memory_space_constraint(adjoint_source, pltpu.HBM)
    p0, old, wc, near, far, depth = pl.pallas_call(
        pack_kernel,
        out_shape=[shape(*block)] * 3 + [shape(2, NZ, TY)] * 2 + [jax.ShapeDtypeStruct((TX, TY), jnp.int32)],
        in_specs=[HBM] * 4,
        out_specs=[VMEM] * 6,
        scratch_shapes=[pltpu.VMEM(flat, F32), pltpu.VMEM(flat, F32), pltpu.VMEM(flat, jnp.int32), pltpu.SemaphoreType.DMA((4,))],
        compiler_params=params,
        name="pack_columns",
    )(*fields)
    far = lax.ppermute(far, "gy", swap_pairs(count_y, 1))
    near = lax.ppermute(near, "gy", swap_pairs(count_y, 0))
    state = shape(ROWS, 2, DEEP, TY)
    sums = shape(STEPS, TX, 8, TY)
    strip_a, strip_b, l0, lold, w, l1, l2, trace = pl.pallas_call(
        edge_kernel,
        out_shape=[shape(STRIP, NZ, TY)] * 2 + [state] * 2 + [shape(ROWS, 2, NZ, TY)] + [state] * 2 + [sums],
        in_specs=[VMEM] * 6 + [SMEM, HBM],
        out_specs=[VMEM] * 8,
        scratch_shapes=SMALL,
        compiler_params=params,
        cost_estimate=cost(24, 10**6),
        name="edge_rows",
    )(p0, old, wc, near, far, depth, sensor_cell, adjoint_source)
    strip_a = lax.ppermute(strip_a, "gx", swap_pairs(count_x, 0))
    strip_b = lax.ppermute(strip_b, "gx", swap_pairs(count_x, 1))
    l1, l2, trace, l3, l4, l5, l6 = pl.pallas_call(
        inner_kernel,
        out_shape=[state] * 2 + [sums] + [state] * 4,
        in_specs=[VMEM] * 7 + [SMEM, HBM],
        out_specs=[VMEM] * 7,
        scratch_shapes=SMALL,
        input_output_aliases={3: 0, 4: 1, 5: 2},
        compiler_params=params,
        cost_estimate=cost(100, 10**6),
        name="inner_rows",
    )(l0, lold, w, l1, l2, trace, depth, sensor_cell, adjoint_source)
    held = [l0, lold, w, l1, l2, l3, l4, l5, l6, trace]
    given = pl.pallas_call(
        frontier_kernel,
        out_shape=[shape(*a.shape) for a in held] + [shape(STEPS * TX, TY), shape(sensors, STEPS * TX, TY)],
        in_specs=[VMEM] * 13 + [SMEM, HBM],
        out_specs=[VMEM] * 12,
        scratch_shapes=SMALL,
        input_output_aliases={i: i for i in range(10)},
        compiler_params=params,
        cost_estimate=cost(100, 10**6),
        name="frontier_rows",
    )(*held, strip_a, strip_b, depth, sensor_cell, adjoint_source)
    final, mine, others = given[8], given[10], given[11]
    others = lax.all_to_all(others, "sensor", 0, 0)
    field, surface = pl.pallas_call(
        give_kernel,
        out_shape=[shape(*flat), shape(TX, TY)],
        in_specs=[VMEM],
        out_specs=[VMEM] * 2,
        compiler_params=params,
        cost_estimate=cost(8, 10**6),
        name="field_rows",
    )(final)
    gram = jnp.sum(mine[None] * others, axis=(1, 2))
    return field.reshape(1, NZ, TX, TY), surface[None], gram.reshape(1, 1, 1, sensors)


def solution(mesh):
    return jax.shard_map(
        on_device,
        mesh=mesh,
        in_specs=(
            P("sensor", None, "gx", "gy"),
            P("sensor", None, "gx", "gy"),
            P("sensor", None),
            P("sensor"),
            P(None, "gx", "gy"),
            P("gx", "gy"),
        ),
        out_specs=(
            P("sensor", None, "gx", "gy"),
            P("sensor", "gx", "gy"),
            P("gx", "gy", "sensor", None),
        ),
        check_vma=False,
    )
```

```python
import functools

import jax
import jax.numpy as jnp
from jax import lax
from jax.experimental import pallas as pl
from jax.experimental.pallas import tpu as pltpu
from jax.sharding import PartitionSpec as P

STEPS = 6
COURANT_SQUARED = (0.08, 0.11, 0.14, 0.17, 0.2, 0.23, 0.26, 0.3)
SURFACE_RATE = 0.3

NZ, TX, TY = 64, 16, 128
HALO = 4
ROWS = TX + 2 * HALO
TOP = 8
DEEP = NZ + 16
CHUNK = 16
STRIP = 11
ITEMS = (("p0", 1), ("p0", 2), ("old", 1), ("p1", 2), ("p1", 3), ("p2", 3), ("wc", 1), ("wc", 2), ("p2", 4), ("wc", 3))
VMEM = pl.BlockSpec(memory_space=pltpu.VMEM)
SMEM = pl.BlockSpec(memory_space=pltpu.SMEM)
HBM = pl.BlockSpec(memory_space=pltpu.HBM)
F32 = jnp.float32


def lanes(rows):
    return lax.broadcasted_iota(jnp.int32, (rows, TY), 1)


def rolled(values, shift):
    shift = shift % TY
    return values if shift == 0 else pltpu.roll(values, shift, axis=1)


def swap_pairs(count, first):
    return [pair for i in range(first, count - 1, 2) for pair in ((i, i + 1), (i + 1, i))]


def pack_kernel(last, prev, kind, depth, p0, old, wc, far, near, depth_out, now_v, prev_v, kind_v, depth_v, sems):
    copies = [
        pltpu.make_async_copy(src, dst, sems.at[i])
        for i, (src, dst) in enumerate(((last, now_v), (prev, prev_v), (kind, kind_v), (depth, depth_v)))
    ]
    for copy in copies:
        copy.start()
    even = lax.rem(lax.axis_index("gy"), 2) == 0
    lane = lanes(NZ)
    level = lax.broadcasted_iota(jnp.int32, (NZ, TY), 0)
    depth_out[...] = jnp.zeros((ROWS, TY), jnp.int32)
    for copy in copies:
        copy.wait()
    depth_out[HALO : HALO + TX, :] = depth_v[...]

    def half(h, carry):
        left = jnp.zeros((NZ, TY), F32)
        right = jnp.zeros((NZ, TY), F32)
        for j in range(8):
            x = h * 8 + j
            here = pl.ds(x, NZ, stride=TX)
            now, before, k = now_v[here, :], prev_v[here, :], kind_v[here, :]
            coef = jnp.full((NZ, TY), COURANT_SQUARED[0], F32)
            for category in range(1, 8):
                coef = jnp.where(k == category, COURANT_SQUARED[category], coef)
            coef = jnp.where(level < depth_v[pl.ds(x, 1), :], coef, 0.0)
            p0[x], old[x], wc[x] = now, before, coef
            base = 16 * j
            for values, start, width in ((now, base, 6), (before, base + 6, 5), (coef, base + 11, 5)):
                mine = (lane >= start) & (lane < start + width)
                left = jnp.where(mine, rolled(values, start), left)
                right = jnp.where(mine, rolled(values, start - (TY - width)), right)
        near[h] = jnp.where(even, right, left)
        far[h] = jnp.where(even, left, right)
        return carry

    lax.fori_loop(0, 2, half, 0)


def update_row(now, old, wc, out, row, depth_row=None, trace=None, tiles=(0, 1)):
    lane = lanes(CHUNK)
    results = []
    total = jnp.zeros((8, TY), F32)
    for start in range(0, NZ, CHUNK):
        at = pl.ds(TOP + start, CHUNK)
        centre = [now[row, t, at, :] for t in (0, 1)]
        for t in tiles:
            left = pltpu.roll(jnp.where(lane == TY - 1, centre[1 - t], centre[t]), 1, axis=1)
            right = pltpu.roll(jnp.where(lane == 0, centre[1 - t], centre[t]), TY - 1, axis=1)
            beside = left + right
            rows = now[row - 1, t, at, :] + now[row + 1, t, at, :]
            levels = now[row, t, pl.ds(TOP + start - 1, CHUNK), :] + now[row, t, pl.ds(TOP + start + 1, CHUNK), :]
            laplace = (rows + beside) + levels - 6.0 * centre[t]
            coef = wc[row, t, pl.ds(start, CHUNK), :]
            fresh = 2.0 * centre[t] - old[row, t, at, :] + coef * laplace
            fresh = jnp.where(coef > 0.0, fresh, 0.0)
            results.append((t, at, fresh))
            if t == 0 and depth_row is not None:
                level = lax.broadcasted_iota(jnp.int32, (CHUNK, TY), 0) + start
                bed = jnp.where(level == depth_row - 1, fresh, 0.0)
                for part in range(0, CHUNK, 8):
                    total = total + bed[part : part + 8]
    top = pl.ds(TOP - 1, 1)
    etas = []
    for t in tiles:
        eta = now[row, t, top, :]
        etas.append(eta + SURFACE_RATE * (results[t][2][0:1] - eta))
    for t, at, fresh in results:
        out[row, t, at, :] = fresh
    for t in tiles:
        out[row, t, top, :] = etas[t]
        out[row, t, TOP + NZ : TOP + NZ + 1, :] = jnp.zeros((1, TY), F32)
    if trace is not None:
        trace[row] = total


def fetch(source, source_s, sem):
    copy = pltpu.make_async_copy(source, source_s, sem)
    copy.start()
    return copy


def sensor_place(cell):
    number = cell[0]
    size_y = TY * lax.axis_size("gy")
    plane = TX * lax.axis_size("gx") * size_y
    z = lax.div(number, plane)
    x = lax.div(lax.rem(number, plane), size_y) - TX * lax.axis_index("gx")
    y = lax.rem(number, size_y) - TY * lax.axis_index("gy")
    tile = jnp.where((y >= 0) & (y < TY), 0, 1)
    lane = lax.rem(y + 2 * size_y, TY)
    return z, x, tile, lane, (y >= -5) & (y < TY + 5)


def inject(out, place, amount, inside, depth, trace):
    z, x, tile, lane, here = place
    hit = jnp.where(lanes(1) == lane, jnp.where(here & inside, amount, 0.0), 0.0)
    row = jnp.clip(x + HALO, 0, ROWS - 1)
    at = pl.ds(TOP + z, 1)
    out[row, tile, at, :] = out[row, tile, at, :] + hit
    top = pl.ds(TOP - 1, 1)
    out[row, tile, top, :] = out[row, tile, top, :] + jnp.where(z == 0, SURFACE_RATE, 0.0) * hit
    bed = (depth[pl.ds(row, 1), :] - 1 == z) & (tile == 0)
    trace[row, 0:1, :] = trace[row, 0:1, :] + jnp.where(bed, hit, 0.0)


def between(x, first, end):
    inner = jnp.minimum(x, TX - 1 - x)
    return (inner >= first) & (inner < end)


def own_rows(now, old, wc, out, first, end, depth, trace, tiles=(0, 1)):
    def pair(x, carry):
        for y in (x, TX - 1 - x):
            update_row(now, old, wc, out, y + HALO, depth[pl.ds(y + HALO, 1), :], trace, tiles)
        return carry

    lax.fori_loop(first, end, pair, 0)


def clear_ends(ref, row, t):
    ref[row, t, 0:TOP, :] = jnp.zeros((TOP, TY), F32)
    ref[row, t, TOP + NZ :, :] = jnp.zeros((8, TY), F32)


def edge_kernel(p0, old, wc, far, near, depth, cell, source, strip_a, strip_b, l0, lold, w, l1, l2, trace,
                source_s, sem):
    copy = fetch(source, source_s, sem)
    even = lax.rem(lax.axis_index("gy"), 2) == 0
    lane = lanes(NZ)
    body = slice(TOP, TOP + NZ)

    def half(h, carry):
        from_right = jnp.where(even, near[h], far[h])
        from_left = jnp.where(even, far[h], near[h])
        for j in range(8):
            x = h * 8 + j
            row = x + HALO
            base = 16 * j
            aux = []
            for start, width in ((base, 6), (base + 6, 5), (base + 11, 5)):
                right = rolled(from_right, -start)
                left = rolled(from_left, TY - width - start)
                aux.append(jnp.where(lane < width, right, jnp.where(lane >= TY - width, left, 0.0)))
            l0[row, 0, body, :], lold[row, 0, body, :], w[row, 0] = p0[x], old[x], wc[x]
            l0[row, 1, body, :], lold[row, 1, body, :], w[row, 1] = aux
            for t in (0, 1):
                clear_ends(l0, row, t)
        return carry

    lax.fori_loop(0, 2, half, 0)
    copy.wait()
    place = sensor_place(cell)
    own_rows(l0, lold, w, l1, 1, 5, depth, trace.at[0])
    inject(l1, place, source_s[0, 0], between(place[1], 1, 5), depth, trace.at[0])
    own_rows(l1, l0, w, l2, 2, 4, depth, trace.at[1])
    inject(l2, place, source_s[0, 1], between(place[1], 2, 4), depth, trace.at[1])

    upper_a = lax.rem(lax.axis_index("gx"), 2) == 0
    for strip, upper in ((strip_a, upper_a), (strip_b, ~upper_a)):
        corner = jnp.zeros((NZ, TY), F32)
        for k, (name, d) in enumerate(ITEMS):
            row = HALO + jnp.where(upper, TX - d, d - 1)
            if name == "wc":
                main, aux = w[row, 0], w[row, 1]
            else:
                ref = {"old": lold, "p0": l0, "p1": l1, "p2": l2}[name]
                main, aux = ref[row, 0, body, :], ref[row, 1, body, :]
            strip[k] = main
            if k < 8:
                corner = jnp.where((lane >= 16 * k) & (lane < 16 * k + 16), rolled(aux, 8 + 16 * k), corner)
        strip[STRIP - 1] = corner


def inner_kernel(l0, lold, w, l1_in, l2_in, trace_in, depth, cell, source, l1, l2, trace, l3, l4, l5, l6,
                 source_s, sem):
    copy = fetch(source, source_s, sem)
    copy.wait()
    place = sensor_place(cell)
    steps = [lold, l0, l1, l2, l3, l4, l5, l6]
    for n, first in zip(range(1, STEPS + 1), (5, 4, 3, 4, 5, 6)):
        now, old, out = steps[n], steps[n - 1], steps[n + 1]
        own_rows(now, old, w, out, first, TX // 2, depth, trace.at[n - 1], (0, 1) if n < STEPS else (0,))
        inject(out, place, source_s[0, n - 1], between(place[1], first, TX // 2), depth, trace.at[n - 1])


def frontier_kernel(facing, last, *refs):
    ins, rest = refs[:14], refs[14:]
    strip, depth, cell, source = ins[10:]
    l0, lold, w, l1, l2, l3, l4, l5, l6, trace = rest[:10]
    source_s, sem = rest[-2:]
    copy = fetch(source, source_s, sem)
    body = slice(TOP, TOP + NZ)
    lane = lanes(NZ)
    top = slice(TOP - 1, TOP)
    upper = lax.rem(lax.axis_index("gx"), 2) == facing

    first, step = jnp.where(upper, HALO + TX - 1, HALO), jnp.where(upper, -1, 1)

    def place_of(i):
        return first + step * i

    corner = strip[STRIP - 1]
    for k, (name, d) in enumerate(ITEMS):
        row = place_of(-d)
        if k < 8:
            aux = jnp.where((lane < 8) | (lane >= TY - 8), rolled(corner, -(8 + 16 * k)), 0.0)
        else:
            aux = jnp.zeros((NZ, TY), F32)
        for t, values in ((0, strip[k]), (1, aux)):
            if name == "wc":
                w[row, t] = values
                continue
            ref = {"old": lold, "p0": l0, "p1": l1, "p2": l2}[name]
            clear_ends(ref, row, t)
            ref[row, t, body, :] = values
            if name == "p1":
                l1[row, t, top, :] = SURFACE_RATE * values[0:1]
            if name == "p2" and d == 3:
                eta = l1[row, t, top, :]
                l2[row, t, top, :] = eta + SURFACE_RATE * (values[0:1] - eta)
    copy.wait()
    place = sensor_place(cell)
    x_s = jnp.where(upper, TX - 1 - place[1], place[1])
    steps = [lold, l0, l1, l2, l3, l4, l5, l6]
    for n, reach in zip(range(1, STEPS + 1), (1, 2, 3, 2, 1, 0)):
        now, old, out = steps[n], steps[n - 1], steps[n + 1]
        half = (n + reach) // 2
        tiles = (0, 1) if n < STEPS else (0,)

        def pair(i, carry):
            for j in (i - reach, i - reach + half):
                row = place_of(j)
                update_row(now, old, w, out, row, depth[pl.ds(row, 1), :], trace.at[n - 1], tiles)
            return carry

        lax.fori_loop(0, half, pair, 0)
        inject(out, place, source_s[0, n - 1], (x_s >= -reach) & (x_s < n), depth, trace.at[n - 1])
    if last:
        mine, others = rest[10:12]
        for n in range(STEPS):
            rows = jnp.sum(trace[n, HALO : HALO + TX], axis=1)
            mine[n * TX : (n + 1) * TX, :] = rows * (1.0 / (STEPS * TX * TY))
            for s in range(others.shape[0]):
                others[s, n * TX : (n + 1) * TX, :] = rows


def give_kernel(final, field, surface):
    def give(x, carry):
        field[pl.ds(x, NZ, stride=TX), :] = final[x + HALO, 0, TOP : TOP + NZ, :]
        surface[pl.ds(x, 1), :] = final[x + HALO, 0, TOP - 1 : TOP, :]
        return carry

    lax.fori_loop(0, TX, give, 0)


def shape(*dims):
    return jax.ShapeDtypeStruct(dims, F32)


def cost(rows, moved):
    return pl.CostEstimate(flops=rows * NZ * TY * 16, bytes_accessed=moved, transcendentals=0)


SMALL = [pltpu.SMEM((1, STEPS), F32), pltpu.SemaphoreType.DMA]


def on_device(adjoint_last, adjoint_prev, adjoint_source, sensor_cell, sound_class, depth_index):
    sensors = lax.axis_size("sensor")
    count_x, count_y = lax.axis_size("gx"), lax.axis_size("gy")
    params = pltpu.CompilerParams(vmem_limit_bytes=8 * 2**20)
    flat = (NZ * TX, TY)
    block = (TX, NZ, TY)
    fields = [a.reshape(flat) for a in (adjoint_last, adjoint_prev, sound_class)]
    fields = [pltpu.with_memory_space_constraint(a, pltpu.HBM) for a in (*fields, depth_index)]
    adjoint_source = pltpu.with_memory_space_constraint(adjoint_source, pltpu.HBM)
    p0, old, wc, far, near, depth = pl.pallas_call(
        pack_kernel,
        out_shape=[shape(*block)] * 3 + [shape(2, NZ, TY)] * 2 + [jax.ShapeDtypeStruct((ROWS, TY), jnp.int32)],
        in_specs=[HBM] * 4,
        out_specs=[VMEM] * 6,
        scratch_shapes=[pltpu.VMEM(flat, F32), pltpu.VMEM(flat, F32), pltpu.VMEM(flat, jnp.int32),
            pltpu.VMEM((TX, TY), jnp.int32), pltpu.SemaphoreType.DMA((4,)),
        ],
        compiler_params=params,
        name="pack_columns",
    )(*fields)
    far = lax.ppermute(far, "gy", swap_pairs(count_y, 1))
    near = lax.ppermute(near, "gy", swap_pairs(count_y, 0))
    state = shape(ROWS, 2, DEEP, TY)
    sums = shape(STEPS, ROWS, 8, TY)
    strip_a, strip_b, l0, lold, w, l1, l2, trace = pl.pallas_call(
        edge_kernel,
        out_shape=[shape(STRIP, NZ, TY)] * 2 + [state] * 2 + [shape(ROWS, 2, NZ, TY)] + [state] * 2 + [sums],
        in_specs=[VMEM] * 6 + [SMEM, HBM],
        out_specs=[VMEM] * 8,
        scratch_shapes=SMALL,
        compiler_params=params,
        cost_estimate=cost(24, 10**6),
        name="edge_rows",
    )(p0, old, wc, far, near, depth, sensor_cell, adjoint_source)
    strip_a = lax.ppermute(strip_a, "gx", swap_pairs(count_x, 0))
    strip_b = lax.ppermute(strip_b, "gx", swap_pairs(count_x, 1))
    l1, l2, trace, l3, l4, l5, l6 = pl.pallas_call(
        inner_kernel,
        out_shape=[state] * 2 + [sums] + [state] * 4,
        in_specs=[VMEM] * 7 + [SMEM, HBM],
        out_specs=[VMEM] * 7,
        scratch_shapes=SMALL,
        input_output_aliases={3: 0, 4: 1, 5: 2},
        compiler_params=params,
        cost_estimate=cost(100, 10**6),
        name="inner_rows",
    )(l0, lold, w, l1, l2, trace, depth, sensor_cell, adjoint_source)
    held = [l0, lold, w, l1, l2, l3, l4, l5, l6, trace]
    for facing, strip in enumerate((strip_a, strip_b)):
        ends = [shape(STEPS * TX, TY), shape(sensors, STEPS * TX, TY)] if facing else []
        held = pl.pallas_call(
            functools.partial(frontier_kernel, facing, bool(facing)),
            out_shape=[shape(*a.shape) for a in held] + ends,
            in_specs=[VMEM] * 12 + [SMEM, HBM],
            out_specs=[VMEM] * (10 + len(ends)),
            scratch_shapes=SMALL,
            input_output_aliases={i: i for i in range(10)},
            compiler_params=params,
            cost_estimate=cost(60, 10**6),
            name="frontier_" + "ab"[facing],
        )(*held, strip, depth, sensor_cell, adjoint_source)
    final, mine, others = held[8], held[10], held[11]
    others = lax.all_to_all(others, "sensor", 0, 0)
    field, surface = pl.pallas_call(
        give_kernel,
        out_shape=[shape(*flat), shape(TX, TY)],
        in_specs=[VMEM],
        out_specs=[VMEM] * 2,
        compiler_params=params,
        cost_estimate=cost(8, 10**6),
        name="field_rows",
    )(final)
    gram = jnp.sum(mine[None] * others, axis=(1, 2))
    return field.reshape(1, NZ, TX, TY), surface[None], gram.reshape(1, 1, 1, sensors)


def solution(mesh):
    return jax.shard_map(
        on_device,
        mesh=mesh,
        in_specs=(
            P("sensor", None, "gx", "gy"),
            P("sensor", None, "gx", "gy"),
            P("sensor", None),
            P("sensor"),
            P(None, "gx", "gy"),
            P("gx", "gy"),
        ),
        out_specs=(
            P("sensor", None, "gx", "gy"),
            P("sensor", "gx", "gy"),
            P("gx", "gy", "sensor", None),
        ),
        check_vma=False,
    )
```

```python
import functools

import jax
import jax.numpy as jnp
from jax import lax
from jax.experimental import pallas as pl
from jax.experimental.pallas import tpu as pltpu
from jax.sharding import PartitionSpec as P

STEPS = 6
COURANT_SQUARED = (0.08, 0.11, 0.14, 0.17, 0.2, 0.23, 0.26, 0.3)
SURFACE_RATE = 0.3

NZ, TX, TY = 64, 16, 128
HALO = 4
ROWS = TX + 2 * HALO
TOP = 8
DEEP = NZ + 16
CHUNK = 16
STRIP = 11
ITEMS = (("p0", 1), ("p0", 2), ("old", 1), ("p1", 2), ("p1", 3), ("p2", 3), ("wc", 1), ("wc", 2), ("p2", 4), ("wc", 3))
VMEM = pl.BlockSpec(memory_space=pltpu.VMEM)
SMEM = pl.BlockSpec(memory_space=pltpu.SMEM)
HBM = pl.BlockSpec(memory_space=pltpu.HBM)
F32 = jnp.float32


def lanes(rows):
    return lax.broadcasted_iota(jnp.int32, (rows, TY), 1)


def rolled(values, shift):
    shift = shift % TY
    return values if shift == 0 else pltpu.roll(values, shift, axis=1)


def swap_pairs(count, first):
    return [pair for i in range(first, count - 1, 2) for pair in ((i, i + 1), (i + 1, i))]


def clear_ends(ref, row, t):
    ref[row, t, 0:TOP, :] = jnp.zeros((TOP, TY), F32)
    ref[row, t, TOP + NZ :, :] = jnp.zeros((8, TY), F32)


PLACES = ((0, 6), (6, 5), (11, 5))


def pack_kernel(last, prev, kind, depth, source, far, near, l0, lold, w, depth_out, amounts,
                now_v, prev_v, kind_v, depth_v, source_v, sems):
    part = NZ // 2
    copies = [pltpu.make_async_copy(depth, depth_v, sems.at[0])]
    for z in (0, 1):
        at = pl.ds(z * part * TX, part * TX)
        for src, dst in ((last, now_v), (prev, prev_v), (kind, kind_v)):
            copies.append(pltpu.make_async_copy(src.at[at], dst.at[at], sems.at[len(copies)]))
    copies.append(pltpu.make_async_copy(source, source_v, sems.at[len(copies)]))
    for copy in copies:
        copy.start()
    even = lax.rem(lax.axis_index("gy"), 2) == 0
    lane = lanes(part)
    spot = lax.rem(lane, 16)
    depth_out[...] = jnp.zeros((ROWS, TY), jnp.int32)
    for x in range(TX):
        for t in (0, 1):
            clear_ends(l0, x + HALO, t)
    copies[0].wait()
    depth_out[HALO : HALO + TX, :] = depth_v[...]
    copies[7].wait()
    amounts[...] = jnp.zeros((8, TY), F32)
    for n in range(STEPS):
        amounts[n : n + 1, :] = jnp.broadcast_to(source_v[0:1, n : n + 1], (1, TY))
    for z in (0, 1):
        for copy in copies[1 + 3 * z : 4 + 3 * z]:
            copy.wait()
        start = z * part
        level = lax.broadcasted_iota(jnp.int32, (part, TY), 0) + start
        for h in (0, 1):
            groups = [jnp.zeros((part, TY), F32)] * 3
            for j in range(8):
                x = h * 8 + j
                here = pl.ds(x + start * TX, part, stride=TX)
                now, before, k = now_v[here, :], prev_v[here, :], kind_v[here, :]
                coef = jnp.full((part, TY), COURANT_SQUARED[0], F32)
                for category in range(1, 8):
                    coef = jnp.where(k == category, COURANT_SQUARED[category], coef)
                coef = jnp.where(level < depth_v[x : x + 1, :], coef, 0.0)
                l0[x + HALO, 0, TOP + start : TOP + start + part, :] = now
                lold[x + HALO, 0, TOP + start : TOP + start + part, :] = before
                w[x + HALO, 0, start : start + part, :] = coef
                for i, (values, (offset, width)) in enumerate(zip((now, before, coef), PLACES)):
                    middle = 16 * j + offset
                    if middle < width:
                        mask = (lane >= TY + middle - width) | (lane < middle + width)
                    else:
                        mask = (lane >= middle - width) & (lane < middle + width)
                    groups[i] = jnp.where(mask, rolled(values, middle), groups[i])
            left = jnp.where(spot < 6, groups[0], jnp.where(spot < 11, groups[1], groups[2]))
            moved = [rolled(group, width) for group, (_, width) in zip(groups, PLACES)]
            right = jnp.where(spot < 6, moved[0], jnp.where(spot < 11, moved[1], moved[2]))
            near[h, start : start + part, :] = jnp.where(even, right, left)
            far[h, start : start + part, :] = jnp.where(even, left, right)


def update_row(now, old, wc, out, row, depth_row=None, trace=None, tiles=(0, 1)):
    lane = lanes(CHUNK)
    results = []
    total = jnp.zeros((8, TY), F32)
    for start in range(0, NZ, CHUNK):
        at = pl.ds(TOP + start, CHUNK)
        centre = [now[row, t, at, :] for t in (0, 1)]
        for t in tiles:
            left = pltpu.roll(jnp.where(lane == TY - 1, centre[1 - t], centre[t]), 1, axis=1)
            right = pltpu.roll(jnp.where(lane == 0, centre[1 - t], centre[t]), TY - 1, axis=1)
            beside = left + right
            rows = now[row - 1, t, at, :] + now[row + 1, t, at, :]
            levels = now[row, t, pl.ds(TOP + start - 1, CHUNK), :] + now[row, t, pl.ds(TOP + start + 1, CHUNK), :]
            laplace = (rows + beside) + levels - 6.0 * centre[t]
            coef = wc[row, t, pl.ds(start, CHUNK), :]
            fresh = 2.0 * centre[t] - old[row, t, at, :] + coef * laplace
            fresh = jnp.where(coef > 0.0, fresh, 0.0)
            results.append((t, at, fresh))
            if t == 0 and depth_row is not None:
                level = lax.broadcasted_iota(jnp.int32, (CHUNK, TY), 0) + start
                bed = jnp.where(level == depth_row - 1, fresh, 0.0)
                for part in range(0, CHUNK, 8):
                    total = total + bed[part : part + 8]
    top = pl.ds(TOP - 1, 1)
    etas = []
    for t in tiles:
        eta = now[row, t, top, :]
        etas.append(eta + SURFACE_RATE * (results[t][2][0:1] - eta))
    for t, at, fresh in results:
        out[row, t, at, :] = fresh
    for t in tiles:
        out[row, t, top, :] = etas[t]
        out[row, t, TOP + NZ : TOP + NZ + 1, :] = jnp.zeros((1, TY), F32)
    if trace is not None:
        trace[row - HALO : row - HALO + 1, :] = jnp.sum(total, axis=0, keepdims=True)


def sensor_place(cell):
    number = cell[0]
    size_y = TY * lax.axis_size("gy")
    plane = TX * lax.axis_size("gx") * size_y
    z = lax.div(number, plane)
    x = lax.div(lax.rem(number, plane), size_y) - TX * lax.axis_index("gx")
    y = lax.rem(number, size_y) - TY * lax.axis_index("gy")
    tile = jnp.where((y >= 0) & (y < TY), 0, 1)
    lane = lax.rem(y + 2 * size_y, TY)
    return z, x, tile, lane, (y >= -5) & (y < TY + 5)


def inject(out, place, amount, inside, depth, trace):
    z, x, tile, lane, here = place
    hit = jnp.where((lanes(1) == lane) & here & inside, amount, 0.0)
    row = jnp.clip(x + HALO, 0, ROWS - 1)
    at = pl.ds(TOP + z, 1)
    out[row, tile, at, :] = out[row, tile, at, :] + hit
    top = pl.ds(TOP - 1, 1)
    out[row, tile, top, :] = out[row, tile, top, :] + jnp.where(z == 0, SURFACE_RATE, 0.0) * hit
    bed = (depth[pl.ds(row, 1), :] - 1 == z) & (tile == 0) & (x >= 0) & (x < TX)
    at = pl.ds(jnp.clip(x, 0, TX - 1), 1)
    trace[at, :] = trace[at, :] + jnp.where(bed, hit, 0.0)


def between(x, first, end):
    inner = jnp.minimum(x, TX - 1 - x)
    return (inner >= first) & (inner < end)


def own_rows(now, old, wc, out, first, end, depth, trace, tiles=(0, 1)):
    for x in range(first, end):
        for row in (x + HALO, TX - 1 - x + HALO):
            update_row(now, old, wc, out, row, depth[row : row + 1, :], trace, tiles)


def unpack(far, near, l0, lold, w, wanted):
    even = lax.rem(lax.axis_index("gy"), 2) == 0
    lane = lanes(NZ)
    spot = lax.rem(lane, 16)
    body = slice(TOP, TOP + NZ)
    for h in (0, 1):
        right = jnp.where(even, near[h], far[h])
        left = jnp.where(even, far[h], near[h])
        left_6, left_5 = rolled(left, -6), rolled(left, -5)
        merged = (
            jnp.where(spot >= 10, left_6, right),
            jnp.where(spot < 6, left_5, right),
            jnp.where(spot < 11, left_5, right),
        )
        for j in range(8):
            if h * 8 + j not in wanted:
                continue
            row = h * 8 + j + HALO
            aux = [
                jnp.where((lane < width) | (lane >= TY - width), rolled(values, -(16 * j + offset)), 0.0)
                for values, (offset, width) in zip(merged, PLACES)
            ]
            l0[row, 1, body, :], lold[row, 1, body, :], w[row, 1] = aux


def edge_kernel(far, near, l0_in, lold_in, w_in, depth, source, cell, strip_a, strip_b, l0, lold, w, l1, l2, trace):
    lane = lanes(NZ)
    body = slice(TOP, TOP + NZ)
    unpack(far, near, l0, lold, w, [*range(6), *range(10, TX)])
    place = sensor_place(cell)
    own_rows(l0, lold, w, l1, 1, 5, depth, trace.at[0])
    inject(l1, place, source[0:1, :], between(place[1], 1, 5), depth, trace.at[0])
    own_rows(l1, l0, w, l2, 2, 4, depth, trace.at[1])
    inject(l2, place, source[1:2, :], between(place[1], 2, 4), depth, trace.at[1])

    upper_a = lax.rem(lax.axis_index("gx"), 2) == 0
    for strip, upper in ((strip_a, upper_a), (strip_b, ~upper_a)):
        corner = jnp.zeros((NZ, TY), F32)
        for k, (name, d) in enumerate(ITEMS):
            row = HALO + jnp.where(upper, TX - d, d - 1)
            if name == "wc":
                main, aux = w[row, 0], w[row, 1]
            else:
                ref = {"old": lold, "p0": l0, "p1": l1, "p2": l2}[name]
                main, aux = ref[row, 0, body, :], ref[row, 1, body, :]
            strip[k] = main
            if k < 8:
                corner = jnp.where((lane >= 16 * k) & (lane < 16 * k + 16), rolled(aux, 8 + 16 * k), corner)
        strip[STRIP - 1] = corner


def inner_kernel(l0_in, lold_in, w_in, l1_in, l2_in, trace_in, far, near, depth, source, cell,
                 l0, lold, w, l1, l2, trace, l3, l4, l5, l6):
    unpack(far, near, l0, lold, w, range(6, 10))
    place = sensor_place(cell)
    steps = [lold, l0, l1, l2, l3, l4, l5, l6]
    for n, first in zip(range(1, STEPS + 1), (5, 4, 3, 4, 5, 6)):
        now, old, out = steps[n], steps[n - 1], steps[n + 1]
        own_rows(now, old, w, out, first, TX // 2, depth, trace.at[n - 1], (0, 1) if n < STEPS else (0,))
        inject(out, place, source[n - 1 : n, :], between(place[1], first, TX // 2), depth, trace.at[n - 1])


def frontier_kernel(facing, *refs):
    upper = lax.rem(lax.axis_index("gx"), 2) == facing

    @pl.when(upper)
    def _():
        frontier_side(True, *refs)

    @pl.when(~upper)
    def _():
        frontier_side(False, *refs)


def frontier_side(upper, *refs):
    strip, depth, source, cell = refs[10:14]
    l0, lold, w, l1, l2, l3, l4, l5, l6, trace, *others = refs[14:]
    body = slice(TOP, TOP + NZ)
    lane = lanes(NZ)
    top = slice(TOP - 1, TOP)

    def place_of(i):
        return HALO + (TX - 1 - i if upper else i)

    corner = strip[STRIP - 1]
    for k, (name, d) in enumerate(ITEMS):
        row = place_of(-d)
        if k < 8:
            aux = jnp.where((lane < 8) | (lane >= TY - 8), rolled(corner, -(8 + 16 * k)), 0.0)
        else:
            aux = jnp.zeros((NZ, TY), F32)
        for t, values in ((0, strip[k]), (1, aux)):
            if name == "wc":
                w[row, t] = values
                continue
            ref = {"old": lold, "p0": l0, "p1": l1, "p2": l2}[name]
            clear_ends(ref, row, t)
            ref[row, t, body, :] = values
            if name == "p1":
                l1[row, t, top, :] = SURFACE_RATE * values[0:1]
            if name == "p2" and d == 3:
                eta = l1[row, t, top, :]
                l2[row, t, top, :] = eta + SURFACE_RATE * (values[0:1] - eta)
    place = sensor_place(cell)
    x_s = TX - 1 - place[1] if upper else place[1]
    steps = [lold, l0, l1, l2, l3, l4, l5, l6]
    for n, reach in zip(range(1, STEPS + 1), (1, 2, 3, 2, 1, 0)):
        now, old, out = steps[n], steps[n - 1], steps[n + 1]
        for i in range(-reach, n):
            row = place_of(i)
            if i < 0:
                update_row(now, old, w, out, row)
            else:
                tiles = (0, 1) if n < STEPS else (0,)
                update_row(now, old, w, out, row, depth[row : row + 1, :], trace.at[n - 1], tiles)
        inject(out, place, source[n - 1 : n, :], (x_s >= -reach) & (x_s < n), depth, trace.at[n - 1])
    if others:
        for n in range(STEPS):
            scaled = trace[n] * (1.0 / (STEPS * TX * TY))
            for s in range(others[0].shape[0]):
                others[0][s, n * TX : (n + 1) * TX, :] = scaled


def give_kernel(final, field, surface):
    def give(x, carry):
        field[pl.ds(x, NZ, stride=TX), :] = final[x + HALO, 0, TOP : TOP + NZ, :]
        surface[pl.ds(x, 1), :] = final[x + HALO, 0, TOP - 1 : TOP, :]
        return carry

    lax.fori_loop(0, TX, give, 0)


def shape(*dims):
    return jax.ShapeDtypeStruct(dims, F32)


def cost(rows, moved):
    return pl.CostEstimate(flops=rows * NZ * TY * 16, bytes_accessed=moved, transcendentals=0)


def on_device(adjoint_last, adjoint_prev, adjoint_source, sensor_cell, sound_class, depth_index):
    sensors = lax.axis_size("sensor")
    count_x, count_y = lax.axis_size("gx"), lax.axis_size("gy")
    params = pltpu.CompilerParams(vmem_limit_bytes=8 * 2**20)
    flat = (NZ * TX, TY)
    block = (TX, NZ, TY)
    fields = [a.reshape(flat) for a in (adjoint_last, adjoint_prev, sound_class)]
    fields = [pltpu.with_memory_space_constraint(a, pltpu.HBM) for a in (*fields, depth_index, adjoint_source)]
    state = shape(ROWS, 2, DEEP, TY)
    sums = shape(STEPS, TX, TY)
    coefs = shape(ROWS, 2, NZ, TY)
    far, near, l0, lold, w, depth, amounts = pl.pallas_call(
        pack_kernel,
        out_shape=[shape(2, NZ, TY)] * 2 + [state] * 2 + [coefs, jax.ShapeDtypeStruct((ROWS, TY), jnp.int32), shape(8, TY)],
        in_specs=[HBM] * 5,
        out_specs=[VMEM] * 7,
        scratch_shapes=[
            pltpu.VMEM(flat, F32), pltpu.VMEM(flat, F32), pltpu.VMEM(flat, jnp.int32),
            pltpu.VMEM((TX, TY), jnp.int32), pltpu.VMEM((1, STEPS), F32), pltpu.SemaphoreType.DMA((8,)),
        ],
        compiler_params=params,
        name="pack_columns",
    )(*fields)
    far = lax.ppermute(far, "gy", swap_pairs(count_y, 1))
    near = lax.ppermute(near, "gy", swap_pairs(count_y, 0))
    strip_a, strip_b, l0, lold, w, l1, l2, trace = pl.pallas_call(
        edge_kernel,
        out_shape=[shape(STRIP, NZ, TY)] * 2 + [state] * 2 + [coefs] + [state] * 2 + [sums],
        in_specs=[VMEM] * 7 + [SMEM],
        out_specs=[VMEM] * 8,
        input_output_aliases={2: 2, 3: 3, 4: 4},
        compiler_params=params,
        cost_estimate=cost(24, 10**6),
        name="edge_rows",
    )(far, near, l0, lold, w, depth, amounts, sensor_cell)
    strip_b = lax.ppermute(strip_b, "gx", swap_pairs(count_x, 1))
    strip_a = lax.ppermute(strip_a, "gx", swap_pairs(count_x, 0))
    l0, lold, w, l1, l2, trace, l3, l4, l5, l6 = pl.pallas_call(
        inner_kernel,
        out_shape=[state] * 2 + [coefs] + [state] * 2 + [sums] + [state] * 4,
        in_specs=[VMEM] * 10 + [SMEM],
        out_specs=[VMEM] * 10,
        input_output_aliases={i: i for i in range(6)},
        compiler_params=params,
        cost_estimate=cost(100, 10**6),
        name="inner_rows",
    )(l0, lold, w, l1, l2, trace, far, near, depth, amounts, sensor_cell)
    held = [l0, lold, w, l1, l2, l3, l4, l5, l6, trace]
    for facing, strip in ((1, strip_b), (0, strip_a)):
        ends = [] if facing else [shape(sensors, STEPS * TX, TY)]
        held = pl.pallas_call(
            functools.partial(frontier_kernel, facing),
            out_shape=[shape(*a.shape) for a in held] + ends,
            in_specs=[VMEM] * 13 + [SMEM],
            out_specs=[VMEM] * (10 + len(ends)),
            input_output_aliases={i: i for i in range(10)},
            compiler_params=params,
            cost_estimate=cost(60, 10**6),
            name="frontier_" + "ab"[facing],
        )(*held, strip, depth, amounts, sensor_cell)
    final, mine = held[8], held[9].reshape(STEPS * TX, TY)
    others = lax.all_to_all(held[10], "sensor", 0, 0)
    field, surface = pl.pallas_call(
        give_kernel,
        out_shape=[shape(*flat), shape(TX, TY)],
        in_specs=[VMEM],
        out_specs=[VMEM] * 2,
        compiler_params=params,
        cost_estimate=cost(8, 10**6),
        name="field_rows",
    )(final)
    gram = jnp.sum(mine[None] * others, axis=(1, 2))
    return field.reshape(1, NZ, TX, TY), surface[None], gram.reshape(1, 1, 1, sensors)


def solution(mesh):
    return jax.shard_map(
        on_device,
        mesh=mesh,
        in_specs=(
            P("sensor", None, "gx", "gy"),
            P("sensor", None, "gx", "gy"),
            P("sensor", None),
            P("sensor"),
            P(None, "gx", "gy"),
            P("gx", "gy"),
        ),
        out_specs=(
            P("sensor", None, "gx", "gy"),
            P("sensor", "gx", "gy"),
            P("gx", "gy", "sensor", None),
        ),
        check_vma=False,
    )
```

```python
import functools

import jax
import jax.numpy as jnp
from jax import lax
from jax.experimental import pallas as pl
from jax.experimental.pallas import tpu as pltpu
from jax.sharding import PartitionSpec as P

STEPS = 6
COURANT_SQUARED = (0.08, 0.11, 0.14, 0.17, 0.2, 0.23, 0.26, 0.3)
SURFACE_RATE = 0.3

NZ, TX, TY = 64, 16, 128
HALO = 4
ROWS = TX + 2 * HALO
TOP = 8
DEEP = NZ + 16
CHUNK = 32
STRIP = 11
ITEMS = (("p0", 1), ("p0", 2), ("old", 1), ("p1", 2), ("p1", 3), ("p2", 3), ("wc", 1), ("wc", 2), ("p2", 4), ("wc", 3))
VMEM = pl.BlockSpec(memory_space=pltpu.VMEM)
SMEM = pl.BlockSpec(memory_space=pltpu.SMEM)
HBM = pl.BlockSpec(memory_space=pltpu.HBM)
F32 = jnp.float32


def lanes(rows):
    return lax.broadcasted_iota(jnp.int32, (rows, TY), 1)


def rolled(values, shift):
    shift = shift % TY
    return values if shift == 0 else pltpu.roll(values, shift, axis=1)


def swap_pairs(count, first):
    return [pair for i in range(first, count - 1, 2) for pair in ((i, i + 1), (i + 1, i))]


def clear_ends(ref, row, t):
    ref[row, t, 0:TOP, :] = jnp.zeros((TOP, TY), F32)
    ref[row, t, TOP + NZ :, :] = jnp.zeros((8, TY), F32)


PLACES = ((0, 6), (6, 5), (11, 5))


def pack_kernel(last, prev, kind, depth, source, far, near, l0, lold, w, depth_out, amounts,
                now_v, prev_v, kind_v, depth_v, source_v, sems):
    part = NZ // 2
    copies = [pltpu.make_async_copy(depth, depth_v, sems.at[0])]
    for z in (0, 1):
        at = pl.ds(z * part * TX, part * TX)
        for src, dst in ((last, now_v), (prev, prev_v), (kind, kind_v)):
            copies.append(pltpu.make_async_copy(src.at[at], dst.at[at], sems.at[len(copies)]))
    copies.append(pltpu.make_async_copy(source, source_v, sems.at[len(copies)]))
    for copy in copies:
        copy.start()
    even = lax.rem(lax.axis_index("gy"), 2) == 0
    lane = lanes(part)
    spot = lax.rem(lane, 16)
    depth_out[...] = jnp.zeros((ROWS, TY), jnp.int32)
    for x in range(TX):
        for t in (0, 1):
            clear_ends(l0, x + HALO, t)
    copies[0].wait()
    depth_out[HALO : HALO + TX, :] = depth_v[...]
    copies[7].wait()
    amounts[...] = jnp.zeros((8, TY), F32)
    for n in range(STEPS):
        amounts[n : n + 1, :] = jnp.broadcast_to(source_v[0:1, n : n + 1], (1, TY))
    for z in (0, 1):
        for copy in copies[1 + 3 * z : 4 + 3 * z]:
            copy.wait()
        start = z * part
        level = lax.broadcasted_iota(jnp.int32, (part, TY), 0) + start
        for h in (0, 1):
            groups = [jnp.zeros((part, TY), F32)] * 3
            for j in range(8):
                x = h * 8 + j
                here = pl.ds(x + start * TX, part, stride=TX)
                now, before, k = now_v[here, :], prev_v[here, :], kind_v[here, :]
                coef = jnp.full((part, TY), COURANT_SQUARED[0], F32)
                for category in range(1, 8):
                    coef = jnp.where(k == category, COURANT_SQUARED[category], coef)
                coef = jnp.where(level < depth_v[x : x + 1, :], coef, 0.0)
                l0[x + HALO, 0, TOP + start : TOP + start + part, :] = now
                lold[x + HALO, 0, TOP + start : TOP + start + part, :] = before
                w[x + HALO, 0, start : start + part, :] = coef
                for i, (values, (offset, width)) in enumerate(zip((now, before, coef), PLACES)):
                    middle = 16 * j + offset
                    if middle < width:
                        mask = (lane >= TY + middle - width) | (lane < middle + width)
                    else:
                        mask = (lane >= middle - width) & (lane < middle + width)
                    groups[i] = jnp.where(mask, rolled(values, middle), groups[i])
            left = jnp.where(spot < 6, groups[0], jnp.where(spot < 11, groups[1], groups[2]))
            moved = [rolled(group, width) for group, (_, width) in zip(groups, PLACES)]
            right = jnp.where(spot < 6, moved[0], jnp.where(spot < 11, moved[1], moved[2]))
            near[h, start : start + part, :] = jnp.where(even, right, left)
            far[h, start : start + part, :] = jnp.where(even, left, right)


def update_row(now, old, wc, out, row, depth_row=None, trace=None, tiles=(0, 1)):
    lane = lanes(CHUNK)
    results = []
    total = jnp.zeros((8, TY), F32)
    for start in range(0, NZ, CHUNK):
        at = pl.ds(TOP + start, CHUNK)
        centre = [now[row, t, at, :] for t in (0, 1)]
        for t in tiles:
            left = pltpu.roll(jnp.where(lane == TY - 1, centre[1 - t], centre[t]), 1, axis=1)
            right = pltpu.roll(jnp.where(lane == 0, centre[1 - t], centre[t]), TY - 1, axis=1)
            beside = left + right
            rows = now[row - 1, t, at, :] + now[row + 1, t, at, :]
            levels = now[row, t, pl.ds(TOP + start - 1, CHUNK), :] + now[row, t, pl.ds(TOP + start + 1, CHUNK), :]
            laplace = (rows + beside) + levels - 6.0 * centre[t]
            coef = wc[row, t, pl.ds(start, CHUNK), :]
            fresh = 2.0 * centre[t] - old[row, t, at, :] + coef * laplace
            fresh = jnp.where(coef > 0.0, fresh, 0.0)
            results.append((t, at, fresh))
            if t == 0 and depth_row is not None:
                level = lax.broadcasted_iota(jnp.int32, (CHUNK, TY), 0) + start
                bed = jnp.where(level == depth_row - 1, fresh, 0.0)
                for part in range(0, CHUNK, 8):
                    total = total + bed[part : part + 8]
    top = pl.ds(TOP - 1, 1)
    etas = []
    for t in tiles:
        eta = now[row, t, top, :]
        etas.append(eta + SURFACE_RATE * (results[t][2][0:1] - eta))
    for t, at, fresh in results:
        out[row, t, at, :] = fresh
    for t in tiles:
        out[row, t, top, :] = etas[t]
        out[row, t, TOP + NZ : TOP + NZ + 1, :] = jnp.zeros((1, TY), F32)
    if trace is not None:
        trace[row - HALO : row - HALO + 1, :] = jnp.sum(total, axis=0, keepdims=True)


def sensor_place(cell):
    number = cell[0]
    size_y = TY * lax.axis_size("gy")
    plane = TX * lax.axis_size("gx") * size_y
    z = lax.div(number, plane)
    x = lax.div(lax.rem(number, plane), size_y) - TX * lax.axis_index("gx")
    y = lax.rem(number, size_y) - TY * lax.axis_index("gy")
    tile = jnp.where((y >= 0) & (y < TY), 0, 1)
    lane = lax.rem(y + 2 * size_y, TY)
    return z, x, tile, lane, (y >= -5) & (y < TY + 5)


def inject(out, place, amount, inside, depth, trace):
    z, x, tile, lane, here = place
    hit = jnp.where((lanes(1) == lane) & here & inside, amount, 0.0)
    row = jnp.clip(x + HALO, 0, ROWS - 1)
    at = pl.ds(TOP + z, 1)
    out[row, tile, at, :] = out[row, tile, at, :] + hit
    top = pl.ds(TOP - 1, 1)
    out[row, tile, top, :] = out[row, tile, top, :] + jnp.where(z == 0, SURFACE_RATE, 0.0) * hit
    bed = (depth[pl.ds(row, 1), :] - 1 == z) & (tile == 0) & (x >= 0) & (x < TX)
    at = pl.ds(jnp.clip(x, 0, TX - 1), 1)
    trace[at, :] = trace[at, :] + jnp.where(bed, hit, 0.0)


def between(x, first, end):
    inner = jnp.minimum(x, TX - 1 - x)
    return (inner >= first) & (inner < end)


def own_rows(now, old, wc, out, first, end, depth, trace, tiles=(0, 1)):
    for x in range(first, end):
        for row in (x + HALO, TX - 1 - x + HALO):
            update_row(now, old, wc, out, row, depth[row : row + 1, :], trace, tiles)


def unpack(far, near, l0, lold, w, wanted):
    even = lax.rem(lax.axis_index("gy"), 2) == 0
    lane = lanes(NZ)
    spot = lax.rem(lane, 16)
    body = slice(TOP, TOP + NZ)
    for h in (0, 1):
        right = jnp.where(even, near[h], far[h])
        left = jnp.where(even, far[h], near[h])
        left_6, left_5 = rolled(left, -6), rolled(left, -5)
        merged = (
            jnp.where(spot >= 10, left_6, right),
            jnp.where(spot < 6, left_5, right),
            jnp.where(spot < 11, left_5, right),
        )
        for j in range(8):
            if h * 8 + j not in wanted:
                continue
            row = h * 8 + j + HALO
            aux = [
                jnp.where((lane < width) | (lane >= TY - width), rolled(values, -(16 * j + offset)), 0.0)
                for values, (offset, width) in zip(merged, PLACES)
            ]
            l0[row, 1, body, :], lold[row, 1, body, :], w[row, 1] = aux


def edge_kernel(far, near, l0_in, lold_in, w_in, depth, source, cell, strip_a, strip_b, l0, lold, w, l1, l2, trace):
    lane = lanes(NZ)
    body = slice(TOP, TOP + NZ)
    unpack(far, near, l0, lold, w, [*range(6), *range(10, TX)])
    place = sensor_place(cell)
    own_rows(l0, lold, w, l1, 1, 5, depth, trace.at[0])
    inject(l1, place, source[0:1, :], between(place[1], 1, 5), depth, trace.at[0])
    own_rows(l1, l0, w, l2, 2, 4, depth, trace.at[1])
    inject(l2, place, source[1:2, :], between(place[1], 2, 4), depth, trace.at[1])

    upper_a = lax.rem(lax.axis_index("gx"), 2) == 0
    for strip, upper in ((strip_a, upper_a), (strip_b, ~upper_a)):
        corner = jnp.zeros((NZ, TY), F32)
        for k, (name, d) in enumerate(ITEMS):
            row = HALO + jnp.where(upper, TX - d, d - 1)
            if name == "wc":
                main, aux = w[row, 0], w[row, 1]
            else:
                ref = {"old": lold, "p0": l0, "p1": l1, "p2": l2}[name]
                main, aux = ref[row, 0, body, :], ref[row, 1, body, :]
            strip[k] = main
            if k < 8:
                corner = jnp.where((lane >= 16 * k) & (lane < 16 * k + 16), rolled(aux, 8 + 16 * k), corner)
        strip[STRIP - 1] = corner


def inner_kernel(l0_in, lold_in, w_in, l1_in, l2_in, trace_in, far, near, depth, source, cell,
                 l0, lold, w, l1, l2, trace, l3, l4, l5, l6):
    unpack(far, near, l0, lold, w, range(6, 10))
    place = sensor_place(cell)
    steps = [lold, l0, l1, l2, l3, l4, l5, l6]
    for n, first in zip(range(1, STEPS + 1), (5, 4, 3, 4, 5, 6)):
        now, old, out = steps[n], steps[n - 1], steps[n + 1]
        own_rows(now, old, w, out, first, TX // 2, depth, trace.at[n - 1], (0, 1) if n < STEPS else (0,))
        inject(out, place, source[n - 1 : n, :], between(place[1], first, TX // 2), depth, trace.at[n - 1])


def frontier_kernel(facing, *refs):
    upper = lax.rem(lax.axis_index("gx"), 2) == facing

    @pl.when(upper)
    def _():
        frontier_side(True, *refs)

    @pl.when(~upper)
    def _():
        frontier_side(False, *refs)


def frontier_side(upper, *refs):
    strip, depth, source, cell = refs[10:14]
    l0, lold, w, l1, l2, l3, l4, l5, l6, trace, *others = refs[14:]
    body = slice(TOP, TOP + NZ)
    lane = lanes(NZ)
    top = slice(TOP - 1, TOP)

    def place_of(i):
        return HALO + (TX - 1 - i if upper else i)

    corner = strip[STRIP - 1]
    for k, (name, d) in enumerate(ITEMS):
        row = place_of(-d)
        if k < 8:
            aux = jnp.where((lane < 8) | (lane >= TY - 8), rolled(corner, -(8 + 16 * k)), 0.0)
        else:
            aux = jnp.zeros((NZ, TY), F32)
        for t, values in ((0, strip[k]), (1, aux)):
            if name == "wc":
                w[row, t] = values
                continue
            ref = {"old": lold, "p0": l0, "p1": l1, "p2": l2}[name]
            clear_ends(ref, row, t)
            ref[row, t, body, :] = values
            if name == "p1":
                l1[row, t, top, :] = SURFACE_RATE * values[0:1]
            if name == "p2" and d == 3:
                eta = l1[row, t, top, :]
                l2[row, t, top, :] = eta + SURFACE_RATE * (values[0:1] - eta)
    place = sensor_place(cell)
    x_s = TX - 1 - place[1] if upper else place[1]
    steps = [lold, l0, l1, l2, l3, l4, l5, l6]
    for n, reach in zip(range(1, STEPS + 1), (1, 2, 3, 2, 1, 0)):
        now, old, out = steps[n], steps[n - 1], steps[n + 1]
        for i in range(-reach, n):
            row = place_of(i)
            if i < 0:
                update_row(now, old, w, out, row)
            else:
                tiles = (0, 1) if n < STEPS else (0,)
                update_row(now, old, w, out, row, depth[row : row + 1, :], trace.at[n - 1], tiles)
        inject(out, place, source[n - 1 : n, :], (x_s >= -reach) & (x_s < n), depth, trace.at[n - 1])
    if others:
        for n in range(STEPS):
            scaled = trace[n] * (1.0 / (STEPS * TX * TY))
            for s in range(others[0].shape[0]):
                others[0][s, n * TX : (n + 1) * TX, :] = scaled


def give_kernel(final, field, surface):
    def give(x, carry):
        field[pl.ds(x, NZ, stride=TX), :] = final[x + HALO, 0, TOP : TOP + NZ, :]
        surface[pl.ds(x, 1), :] = final[x + HALO, 0, TOP - 1 : TOP, :]
        return carry

    lax.fori_loop(0, TX, give, 0)


def shape(*dims):
    return jax.ShapeDtypeStruct(dims, F32)


def cost(rows, moved):
    return pl.CostEstimate(flops=rows * NZ * TY * 16, bytes_accessed=moved, transcendentals=0)


def on_device(adjoint_last, adjoint_prev, adjoint_source, sensor_cell, sound_class, depth_index):
    sensors = lax.axis_size("sensor")
    count_x, count_y = lax.axis_size("gx"), lax.axis_size("gy")
    params = pltpu.CompilerParams(vmem_limit_bytes=8 * 2**20)
    flat = (NZ * TX, TY)
    block = (TX, NZ, TY)
    fields = [a.reshape(flat) for a in (adjoint_last, adjoint_prev, sound_class)]
    fields = [pltpu.with_memory_space_constraint(a, pltpu.HBM) for a in (*fields, depth_index, adjoint_source)]
    state = shape(ROWS, 2, DEEP, TY)
    sums = shape(STEPS, TX, TY)
    coefs = shape(ROWS, 2, NZ, TY)
    far, near, l0, lold, w, depth, amounts = pl.pallas_call(
        pack_kernel,
        out_shape=[shape(2, NZ, TY)] * 2 + [state] * 2 + [coefs, jax.ShapeDtypeStruct((ROWS, TY), jnp.int32), shape(8, TY)],
        in_specs=[HBM] * 5,
        out_specs=[VMEM] * 7,
        scratch_shapes=[
            pltpu.VMEM(flat, F32), pltpu.VMEM(flat, F32), pltpu.VMEM(flat, jnp.int32),
            pltpu.VMEM((TX, TY), jnp.int32), pltpu.VMEM((1, STEPS), F32), pltpu.SemaphoreType.DMA((8,)),
        ],
        compiler_params=params,
        name="pack_columns",
    )(*fields)
    far = lax.ppermute(far, "gy", swap_pairs(count_y, 1))
    near = lax.ppermute(near, "gy", swap_pairs(count_y, 0))
    strip_a, strip_b, l0, lold, w, l1, l2, trace = pl.pallas_call(
        edge_kernel,
        out_shape=[shape(STRIP, NZ, TY)] * 2 + [state] * 2 + [coefs] + [state] * 2 + [sums],
        in_specs=[VMEM] * 7 + [SMEM],
        out_specs=[VMEM] * 8,
        input_output_aliases={2: 2, 3: 3, 4: 4},
        compiler_params=params,
        cost_estimate=cost(24, 10**6),
        name="edge_rows",
    )(far, near, l0, lold, w, depth, amounts, sensor_cell)
    strip_b = lax.ppermute(strip_b, "gx", swap_pairs(count_x, 1))
    strip_a = lax.ppermute(strip_a, "gx", swap_pairs(count_x, 0))
    l0, lold, w, l1, l2, trace, l3, l4, l5, l6 = pl.pallas_call(
        inner_kernel,
        out_shape=[state] * 2 + [coefs] + [state] * 2 + [sums] + [state] * 4,
        in_specs=[VMEM] * 10 + [SMEM],
        out_specs=[VMEM] * 10,
        input_output_aliases={i: i for i in range(6)},
        compiler_params=params,
        cost_estimate=cost(100, 10**6),
        name="inner_rows",
    )(l0, lold, w, l1, l2, trace, far, near, depth, amounts, sensor_cell)
    held = [l0, lold, w, l1, l2, l3, l4, l5, l6, trace]
    for facing, strip in ((1, strip_b), (0, strip_a)):
        ends = [] if facing else [shape(sensors, STEPS * TX, TY)]
        held = pl.pallas_call(
            functools.partial(frontier_kernel, facing),
            out_shape=[shape(*a.shape) for a in held] + ends,
            in_specs=[VMEM] * 13 + [SMEM],
            out_specs=[VMEM] * (10 + len(ends)),
            input_output_aliases={i: i for i in range(10)},
            compiler_params=params,
            cost_estimate=cost(60, 10**6),
            name="frontier_" + "ab"[facing],
        )(*held, strip, depth, amounts, sensor_cell)
    final, mine = held[8], held[9].reshape(STEPS * TX, TY)
    others = lax.all_to_all(held[10], "sensor", 0, 0)
    field, surface = pl.pallas_call(
        give_kernel,
        out_shape=[shape(*flat), shape(TX, TY)],
        in_specs=[VMEM],
        out_specs=[VMEM] * 2,
        compiler_params=params,
        cost_estimate=cost(8, 10**6),
        name="field_rows",
    )(final)
    gram = jnp.sum(mine[None] * others, axis=(1, 2))
    return field.reshape(1, NZ, TX, TY), surface[None], gram.reshape(1, 1, 1, sensors)


def solution(mesh):
    return jax.shard_map(
        on_device,
        mesh=mesh,
        in_specs=(
            P("sensor", None, "gx", "gy"),
            P("sensor", None, "gx", "gy"),
            P("sensor", None),
            P("sensor"),
            P(None, "gx", "gy"),
            P("gx", "gy"),
        ),
        out_specs=(
            P("sensor", None, "gx", "gy"),
            P("sensor", "gx", "gy"),
            P("gx", "gy", "sensor", None),
        ),
        check_vma=False,
    )
```
